32 devices in a mesh: ch: 4 (over y, x), xy: 8 (over z, core).
Axes of the slice: x: 2, y: 2, z: 4, core: 2. Of those that a mesh axis runs over, the one named last changes fastest.
Arguments:
- inputs: bfloat16 [384, 1, 64, 128], P('ch', None, 'xy'), may hold values from -6 to 6
- weight: bfloat16 [9, 384, 384], P(None, 'ch'), may hold values from -0.125 to 0.125
- bias: float32 [384], P('ch'), may hold values from -3 to 3
- cotangent: bfloat16 [384, 1, 64, 128], P('ch', None, 'xy'), may hold values from -6 to 6
Outputs:
- output: bfloat16 [384, 1, 64, 128], P('ch', None, 'xy')
- grad_inputs: bfloat16 [384, 1, 64, 128], P('ch', None, 'xy')
- grad_weight: float32 [9, 384, 384], P(None, 'ch')
- grad_bias: float32 [384], P('ch')
The draws below stay inside these ranges and needn't reach their ends.
All inputs are finite; a program needn't handle non-finite values.
Results may differ from the reference program's by a relative error of at most 0.0095.
Values may be sent and summed in bfloat16 or wider, within the bound.
A program may use at most 64 MiB of HBM per device.

```python
import jax
import jax.numpy as jnp
from jax import lax

CI = 384
CO = 384
DEPTH = 1
WIDE = 128
ROWS = 64


def with_spikes(result, stream_key, source, target, shards_of, factor):
    owner, partner = [(jnp.arange(result.shape[dim]) // (result.shape[dim] // shards_of)).reshape([-1 if axis == dim else 1 for axis in range(result.ndim)]) for dim in (source, target)]
    chosen = jax.random.permutation(stream_key, shards_of)[partner]
    strong = (owner == chosen) | (owner == (partner + shards_of // 2) % shards_of)
    return jnp.where(strong, factor * result, result)


def levels(own_key, extent, shards, least, high):
    def one(dim, parts):
        heights = jax.random.uniform(jax.random.fold_in(jax.random.fold_in(own_key, 6), dim), (parts,), jnp.float32, least / len(shards), high / len(shards))
        return jnp.repeat(jnp.exp(heights), extent[dim] // parts).reshape((-1,) + (1,) * (len(extent) - dim - 1))

    factor_of = one(*shards[0])
    for cut in shards[1:]:
        factor_of = factor_of * one(*cut)
    return factor_of


def scatter_about(rng, extent, deviation, bound, shards=(), held_as=jnp.bfloat16):
    level = levels(rng, extent, shards, -0.22, 0.18) if shards else 1.0
    values = jax.random.normal(rng, extent, jnp.float32) * deviation * level
    return jnp.minimum(jnp.maximum(values, -bound), bound).astype(held_as)


def gaussian_with(rng, shape, scale, reach, cuts, heavy, kind=jnp.bfloat16):
    drawn = scale * jax.random.normal(rng, shape, jnp.float32)
    if cuts:
        drawn = drawn * levels(rng, shape, cuts, -0.22, 0.18)
    return jnp.clip(with_spikes(drawn, jax.random.fold_in(rng, 3), *heavy), -reach, reach).astype(kind)


def setup_inputs(seed: int = 0) -> dict:
    seeds = jax.random.split(jax.random.key(seed), 5)
    inputs = scatter_about(seeds[0], (CI, DEPTH, ROWS, WIDE), 1.0, 6.0, ((0, 4), (2, 8)))
    weight = gaussian_with(seeds[1], (9, CI, CO), (9 * CI) ** -0.5, 0.125, ((1, 4),), (1, 2, 4, 2.0))
    bias = scatter_about(seeds[2], (CO,), 0.5, 3.0, ((0, 4),), jnp.float32)
    cotangent = scatter_about(seeds[3], (CO, DEPTH, ROWS, WIDE), 1.0, 6.0, ((0, 4), (2, 8)))
    return {"inputs": inputs, "weight": weight, "bias": bias, "cotangent": cotangent}


def tap_offsets():
    return [(a, b) for a in (-1, 0, 1) for b in (-1, 0, 1)]

def contract_lead(left, right):
    return lax.dot_general(left, right, (((0,), (0,)), ((), ())), preferred_element_type=jnp.float32)

def contract_last(left, right):
    return lax.dot_general(left, right, (((1,), (1,)), ((), ())), preferred_element_type=jnp.float32)

def reference(inputs, weight, bias, cotangent):
    chans, depth, rows, wide = inputs.shape
    x_pad = jnp.pad(inputs, ((0, 0), (0, 0), (2, 2), (2, 2)))
    pre = jnp.zeros((CO, depth * rows * wide), jnp.float32)
    for t, (a, b) in enumerate(tap_offsets()):
        window = x_pad[:, :, 2 + 2 * a:2 + 2 * a + rows, 2 + 2 * b:2 + 2 * b + wide].reshape(chans, -1)
        pre = pre + contract_lead(weight[t], window)
    pre = pre + bias[:, None]
    output = jax.nn.gelu(pre, approximate=True).astype(jnp.bfloat16)
    _, pull = jax.vjp(lambda v: jax.nn.gelu(v, approximate=True), pre)
    grad_pre = pull(cotangent.reshape(CO, -1).astype(jnp.float32))[0].astype(jnp.bfloat16)
    g_pad = jnp.pad(grad_pre.reshape(CO, depth, rows, wide), ((0, 0), (0, 0), (2, 2), (2, 2)))
    grad_x = jnp.zeros((chans, depth * rows * wide), jnp.float32)
    grads_w = []
    for t, (a, b) in enumerate(tap_offsets()):
        g_win = g_pad[:, :, 2 - 2 * a:2 - 2 * a + rows, 2 - 2 * b:2 - 2 * b + wide].reshape(CO, -1)
        grad_x = grad_x + jnp.dot(weight[t], g_win, preferred_element_type=jnp.float32)
        window = x_pad[:, :, 2 + 2 * a:2 + 2 * a + rows, 2 + 2 * b:2 + 2 * b + wide].reshape(chans, -1)
        grads_w.append(contract_last(window, grad_pre))
    grad_weight = jnp.stack(grads_w, 0)
    grad_bias = lax.optimization_barrier(jnp.sum(grad_pre.astype(jnp.float32), axis=1))
    return (output.reshape(CO, depth, rows, wide), grad_x.astype(jnp.bfloat16).reshape(chans, depth, rows, wide), grad_weight, grad_bias)
```

```python
import functools
import math

import jax
import jax.numpy as jnp
from jax import lax
from jax.experimental import pallas as pl
from jax.experimental.pallas import tpu as pltpu
from jax.sharding import PartitionSpec as P


def with_halo(shard, sides, width):
    for axis, dim in sides:
        devices, length = (lax.axis_size(axis), shard.shape[dim])
        up = [(i, (i + 1) % devices) for i in range(devices - 1)]
        down = [(j, i) for i, j in up]
        last = lax.slice_in_dim(shard, length - width, length, axis=dim)
        leading = lax.slice_in_dim(shard, 0, width, axis=dim)
        before = lax.ppermute(last, axis, up)
        after = lax.ppermute(leading, axis, down)
        shard = jnp.concatenate([before, shard, after], axis=dim)
    return shard


def tap_offsets():
    return [(a, b) for a in (-1, 0, 1) for b in (-1, 0, 1)]


def pad_columns(block):
    return jnp.pad(block, ((0, 0), (0, 0), (0, 0), (2, 2)))


def window_of(padded, a, b, rows, wide):
    count = padded.shape[0]
    return padded[:, :, 2 + 2 * a : 2 + 2 * a + rows, 2 + 2 * b : 2 + 2 * b + wide].reshape(
        count, -1
    )


def contract_lead(left, right):
    return lax.dot_general(
        left, right, (((0,), (0,)), ((), ())), preferred_element_type=jnp.float32
    )


def contract_last(left, right):
    return lax.dot_general(
        left, right, (((1,), (1,)), ((), ())), preferred_element_type=jnp.float32
    )


def activate(pre, cot_flat):
    output = jax.nn.gelu(pre, approximate=True).astype(jnp.bfloat16)
    _, pull = jax.vjp(lambda v: jax.nn.gelu(v, approximate=True), pre)
    grad_pre = pull(cot_flat.astype(jnp.float32))[0].astype(jnp.bfloat16)
    return (output, grad_pre)


def per_device(inputs, weight, bias, cotangent):
    chans, depth, rows, wide = inputs.shape
    out_local = bias.shape[0]
    cells = depth * rows * wide
    x_rim = with_halo(inputs, (("xy", 2),), 2)
    x_pad = pad_columns(x_rim)
    total = jnp.zeros((lax.axis_size("ch") * out_local, cells), jnp.float32)
    for t, (term_a, term_b) in enumerate(tap_offsets()):
        total = total + contract_lead(weight[t], window_of(x_pad, term_a, term_b, rows, wide))
    pre = lax.psum_scatter(
        total.reshape(lax.axis_size("ch") * out_local, depth, rows, wide),
        "ch",
        scatter_dimension=0,
        tiled=True,
    ).reshape(out_local, cells)
    pre = pre + bias[:, None]
    out_flat, grad_pre = activate(pre, cotangent.reshape(out_local, -1))
    g_rim = with_halo(grad_pre.reshape(out_local, depth, rows, wide), (("xy", 2),), 2)
    windows = [window_of(x_pad, a, b, rows, wide) for a, b in tap_offsets()]
    piece = lax.all_gather(g_rim, "ch", axis=0, tiled=True)
    grad_acc = jnp.zeros((chans, cells), jnp.float32)
    count = piece.shape[0]
    padded = pad_columns(piece)
    center = piece[:, :, 2 : 2 + rows, :].reshape(count, -1)
    pieces_w = []
    for t, (a, b) in enumerate(tap_offsets()):
        w_block = weight[t]
        g_win = padded[:, :, 2 - 2 * a : 2 - 2 * a + rows, 2 - 2 * b : 2 - 2 * b + wide].reshape(
            count, -1
        )
        grad_acc = grad_acc + jnp.dot(w_block, g_win, preferred_element_type=jnp.float32)
        pieces_w.append(contract_last(windows[t], center))
    fresh = jnp.stack(pieces_w, 0)
    grad_acc, grad_w = (grad_acc, fresh)
    grad_b = jnp.sum(grad_pre.astype(jnp.float32), axis=1)
    output = out_flat.reshape(out_local, depth, rows, wide)
    grad_x = grad_acc.astype(jnp.bfloat16).reshape(chans, depth, rows, wide)
    grad_w, grad_b = lax.psum((grad_w, grad_b), "xy")
    return (output, grad_x, grad_w, grad_b)


F32 = jnp.float32
BF16 = jnp.bfloat16
SLOPE = math.sqrt(2.0 / math.pi)


def fused_kernel(
    nch, nxy, x_ref, w_ref, b_ref, cot_ref,
    out_ref, gx_ref, gw_ref, gb_ref,
    xrow, crow, orow, x2d, xim, pf, pb, prv, g2d, sacc,
    gwf, csend, crecv, zsend, zrecv, fin,
    xs, xr, ps, pr, gs, gr, hs, hr, cs, cr, zs, zr, as_, ar, fs, fr,
):
    cl, rows, wide = x_ref.shape
    co = w_ref.shape[1]
    cells = rows * wide
    rim = 2 * wide
    half = cells // 2
    kc = 9 * cl
    me = lax.axis_index("ch")
    xy = lax.axis_index("xy")
    core = lax.rem(xy, 2)
    nz = nxy // 2
    z = xy // 2
    hr_rows = crecv.shape[0]
    shard = hr_rows // nz
    part = kc // 2

    def peer(d):
        return lax.rem(me + d, nch)

    def zpeer(d):
        return lax.rem(z + d, nz) * 2 + core

    def remote(src, dst, ssem, rsem, **where):
        return pltpu.make_async_remote_copy(
            src_ref=src, dst_ref=dst, send_sem=ssem, recv_sem=rsem,
            device_id=where, device_id_type=pl.DeviceIdType.MESH,
        )

    barrier = pltpu.get_barrier_semaphore()
    for d in range(1, nch):
        pl.semaphore_signal(barrier, inc=1, device_id={"ch": peer(d)}, device_id_type=pl.DeviceIdType.MESH)
    for d in range(1, nxy):
        pl.semaphore_signal(
            barrier, inc=1, device_id={"xy": lax.rem(xy + d, nxy)}, device_id_type=pl.DeviceIdType.MESH
        )

    up = xy > 0
    down = xy < nxy - 1

    xrow[...] = x_ref[...].astype(F32).reshape(cl * rows, wide)
    crow[...] = cot_ref[...].astype(F32).reshape(cl * rows, wide)
    for r in range(rows):
        x2d[:, rim + r * wide : rim + (r + 1) * wide] = xrow[pl.ds(r, cl, stride=rows), :].astype(BF16)

    pl.semaphore_wait(barrier, nch - 1 + nxy - 1)

    to_up = remote(x2d.at[:, pl.ds(rim, rim)], x2d.at[:, pl.ds(rim + cells, rim)], xs.at[0], xr.at[0], xy=jnp.maximum(xy - 1, 0))
    to_down = remote(x2d.at[:, pl.ds(cells, rim)], x2d.at[:, pl.ds(0, rim)], xs.at[1], xr.at[1], xy=jnp.minimum(xy + 1, nxy - 1))
    pl.when(up)(to_up.start)
    pl.when(down)(to_down.start)

    lane = lax.broadcasted_iota(jnp.int32, (cl, wide), 1)

    def spread(src_row):
        v = x2d[:, src_row * wide : (src_row + 1) * wide]
        vf = v.astype(F32)
        minus = jnp.where(lane >= 2, pltpu.roll(vf, 2, 1), 0.0).astype(BF16)
        plus = jnp.where(lane < wide - 2, pltpu.roll(vf, wide - 2, 1), 0.0).astype(BF16)
        for a in (-1, 0, 1):
            r = src_row - 2 - 2 * a
            if 0 <= r < rows:
                for b, val in ((-1, minus), (0, v), (1, plus)):
                    t = 3 * (a + 1) + b + 1
                    xim[t * cl : (t + 1) * cl, r * wide : (r + 1) * wide] = val

    for src_row in range(2, rows + 2):
        spread(src_row)
    xim[kc:, :] = jnp.ones((xim.shape[0] - kc, cells), BF16)

    def edge_zero(cond, ref, start):
        @pl.when(jnp.logical_not(cond))
        def _():
            ref[:, start : start + rim] = jnp.zeros((ref.shape[0], rim), BF16)

    edge_zero(up, x2d, 0)
    edge_zero(down, x2d, rim + cells)
    edge_zero(up, g2d, 0)
    edge_zero(down, g2d, rim + cells)

    eye = lax.broadcasted_iota(jnp.int32, (cl, cl), 0) == lax.broadcasted_iota(jnp.int32, (cl, cl), 1)
    bias = jnp.sum(jnp.where(eye, jnp.broadcast_to(b_ref[...], (cl, cl)), 0.0), axis=1, keepdims=True)

    pl.when(up)(to_down.wait_recv)
    pl.when(down)(to_up.wait_recv)
    for src_row in (0, 1, rows + 2, rows + 3):
        spread(src_row)

    own = pl.ds(pl.multiple_of(me * cl, 16), cl)
    psends = []
    for h in range(2):
        cols = pl.ds(h * half, half)
        val = contract_lead(w_ref[...], xim[:kc, h * half : (h + 1) * half])
        pf[:, cols] = val
        pb[:, cols] = val.astype(BF16)
        for d in range(1, nch):
            there = pl.ds(pl.multiple_of(peer(d) * cl, 16), cl)
            k = h * (nch - 1) + d - 1
            c = remote(pb.at[there, cols], prv.at[d - 1, :, cols], ps.at[k], pr.at[k], ch=peer(d))
            c.start()
            psends.append(c)

    gsends = []
    hsends = {}

    def halo_sends(d, which):
        blk = pl.ds(pl.multiple_of(lax.rem(me - d + nch, nch) * cl, 16), cl)
        if which == 0:
            c = remote(
                g2d.at[blk, pl.ds(rim, rim)], g2d.at[blk, pl.ds(rim + cells, rim)],
                hs.at[d], hr.at[d], xy=jnp.maximum(xy - 1, 0),
            )
            pl.when(up)(c.start)
        else:
            c = remote(
                g2d.at[blk, pl.ds(cells, rim)], g2d.at[blk, pl.ds(0, rim)],
                hs.at[nch + d], hr.at[nch + d], xy=jnp.minimum(xy + 1, nxy - 1),
            )
            pl.when(down)(c.start)
        hsends[(d, which)] = c

    for h in range(2):
        cols = pl.ds(h * half, half)
        for d in range(1, nch):
            psends[h * (nch - 1) + d - 1].wait_recv()
        for r in range(h * rows // 2, (h + 1) * rows // 2):
            rc = pl.ds(r * wide, wide)
            v = pf[own, rc] + bias
            for d in range(1, nch):
                v = v + prv[d - 1, :, rc].astype(F32)
            sq = v * v
            th = jnp.tanh(SLOPE * (v + 0.044715 * (sq * v)))
            hp = 0.5 * (1.0 + th)
            orow[pl.ds(r, cl, stride=rows), :] = v * hp
            slope = hp + 0.5 * v * (1.0 - th * th) * (SLOPE * (1.0 + 3.0 * 0.044715 * sq))
            g = crow[pl.ds(r, cl, stride=rows), :] * slope
            g2d[own, pl.ds(rim + r * wide, wide)] = g.astype(BF16)
        for d in range(1, nch):
            k = h * (nch - 1) + d - 1
            blk = g2d.at[own, pl.ds(rim + h * half, half)]
            c = remote(blk, blk, gs.at[k], gr.at[k], ch=peer(d))
            c.start()
            gsends.append(c)
        halo_sends(0, h)

    out_ref[...] = orow[...].reshape(cl, rows, wide).astype(BF16)

    for h in range(2):
        for d in range(1, nch):
            gsends[h * (nch - 1) + d - 1].wait_recv()
            halo_sends(d, h)

    gwf[...] = contract_last(xim[...], g2d[:, rim : rim + cells])
    theirs = pl.ds(pl.multiple_of((1 - core) * part, 16), hr_rows)
    mine = pl.ds(pl.multiple_of(core * part, 16), hr_rows)
    csend[...] = gwf[theirs, :].astype(BF16)
    partner = xy + 1 - 2 * core
    ccopy = remote(csend, crecv, cs.at[0], cr.at[0], xy=partner)
    ccopy.start()

    for d in range(nch):
        pl.when(up)(hsends[(d, 1)].wait_recv)
        pl.when(down)(hsends[(d, 0)].wait_recv)

    pairs = rows // 2
    group = 3 * cl

    def gi_chunk(k, first):
        val = jnp.dot(w_ref[...], g2d[:, k * rim : (k + 1) * rim], preferred_element_type=F32)
        for a in (-1, 0, 1):
            q = k - 1 + a
            if 0 <= q < pairs:
                piece = val[(a + 1) * group : (a + 2) * group]
                if q in first:
                    sacc[:, q * rim : (q + 1) * rim] += piece
                else:
                    first.add(q)
                    sacc[:, q * rim : (q + 1) * rim] = piece

    seen = set()
    for k in range(2):
        gi_chunk(k, seen)

    ccopy.wait_recv()
    mysum = gwf[mine, :] + crecv[...].astype(F32)
    gwf[mine, :] = mysum
    zsend[...] = mysum.astype(BF16)
    zcopies = []
    for d in range(1, nz):
        at = pl.ds(pl.multiple_of(lax.rem(z + d, nz) * shard, 16), shard)
        c = remote(zsend.at[at, :], zrecv.at[d - 1], zs.at[d - 1], zr.at[d - 1], xy=zpeer(d))
        c.start()
        zcopies.append(c)

    for k in range(2, pairs + 2):
        gi_chunk(k, seen)
    for r in range(rows):
        rc = slice(r * wide, (r + 1) * wide)
        v = sacc[cl : 2 * cl, rc]
        v = v + jnp.where(lane < wide - 2, pltpu.roll(sacc[:cl, rc], wide - 2, 1), 0.0)
        v = v + jnp.where(lane >= 2, pltpu.roll(sacc[2 * cl :, rc], 2, 1), 0.0)
        xrow[pl.ds(r, cl, stride=rows), :] = v
    gx_ref[...] = xrow[...].reshape(cl, rows, wide).astype(BF16)

    for c in zcopies:
        c.wait_recv()
    total = gwf[pl.ds(pl.multiple_of(core * part + z * shard, 16), shard), :]
    for d in range(1, nz):
        total = total + zrecv[d - 1].astype(F32)
    sh = pl.ds(pl.multiple_of(z * shard, 16), shard)
    fin[core, sh, :] = total.astype(BF16)
    acopies = []
    fcopies = []
    blk = fin.at[core, sh, :]
    fcopies.append(remote(blk, blk, fs.at[0], fr.at[0], xy=partner))
    for d in range(1, nz):
        c = remote(blk, blk, as_.at[d - 1], ar.at[d - 1], xy=zpeer(d))
        c.start()
        acopies.append(c)
    fcopies[0].start()
    for d in range(1, nz):
        acopies[d - 1].wait_recv()
        src = pl.ds(pl.multiple_of(lax.rem(z - d + nz, nz) * shard, 16), shard)
        blk = fin.at[core, src, :]
        c = remote(blk, blk, fs.at[d], fr.at[d], xy=partner)
        c.start()
        fcopies.append(c)
    for c in fcopies:
        c.wait_recv()
    gw_ref[:part, :] = fin[0, :part, :].astype(F32)
    gw_ref[part:, :] = fin[1, :part, :].astype(F32)
    pick = (
        lax.broadcasted_iota(jnp.int32, (co, wide), 0) == lax.broadcasted_iota(jnp.int32, (co, wide), 1) + me * cl
    ).astype(F32).astype(BF16)
    gb = jnp.dot(fin[1, part:, :], pick, preferred_element_type=F32)
    gb_ref[...] = gb[0:1, :cl]

    pl.when(up)(to_up.wait_send)
    pl.when(down)(to_down.wait_send)
    for c in psends + gsends + zcopies + acopies + fcopies + [ccopy]:
        c.wait_send()
    for d in range(nch):
        pl.when(up)(hsends[(d, 0)].wait_send)
        pl.when(down)(hsends[(d, 1)].wait_send)


def fits(chans, depth, rows, wide, nxy):
    part = 9 * chans // 2
    return (
        depth == 1
        and rows % 4 == 0
        and wide == 128
        and chans % 32 == 0
        and chans <= wide
        and nxy % 2 == 0
        and (part + 16) % (16 * (nxy // 2)) == 0
    )


def layer(inputs, weight, bias, cotangent):
    chans, depth, rows, wide = inputs.shape
    nch, nxy = lax.axis_size("ch"), lax.axis_size("xy")
    if not fits(chans, depth, rows, wide, nxy):
        return per_device(inputs, weight, bias, cotangent)
    co = weight.shape[2]
    cells = rows * wide
    kc = 9 * chans
    nz = nxy // 2
    hrows = kc // 2 + 16
    dma = pltpu.SemaphoreType.DMA
    vmem = pltpu.VMEM
    sems = [2, 2] + [2 * (nch - 1)] * 4 + [2 * nch] * 2 + [1, 1] + [nz - 1] * 4 + [nz, nz]
    out, gx, gw, gb = pl.pallas_call(
        functools.partial(fused_kernel, nch, nxy),
        out_shape=(
            jax.ShapeDtypeStruct((chans, rows, wide), BF16),
            jax.ShapeDtypeStruct((chans, rows, wide), BF16),
            jax.ShapeDtypeStruct((kc, co), F32),
            jax.ShapeDtypeStruct((1, chans), F32),
        ),
        in_specs=[pl.BlockSpec(memory_space=vmem)] * 4,
        out_specs=[pl.BlockSpec(memory_space=vmem)] * 4,
        scratch_shapes=[
            vmem((chans * rows, wide), F32),
            vmem((chans * rows, wide), F32),
            vmem((chans * rows, wide), F32),
            vmem((chans, cells + 4 * wide), BF16),
            vmem((kc + 16, cells), BF16),
            vmem((co, cells), F32),
            vmem((co, cells), BF16),
            vmem((nch - 1, chans, cells), BF16),
            vmem((co, cells + 4 * wide), BF16),
            vmem((3 * chans, cells), F32),
            vmem((kc + 16, co), F32),
            vmem((hrows, co), BF16),
            vmem((hrows, co), BF16),
            vmem((hrows, co), BF16),
            vmem((nz - 1, hrows // nz, co), BF16),
            vmem((2, hrows, co), BF16),
        ]
        + [dma((n,)) for n in sems],
        compiler_params=pltpu.CompilerParams(
            collective_id=0, has_side_effects=True, vmem_limit_bytes=48 * 1024 * 1024
        ),
    )(
        inputs.reshape(chans, rows, wide),
        weight.reshape(kc, co),
        bias.reshape(1, chans),
        cotangent.reshape(chans, rows, wide),
    )
    return (
        out.reshape(chans, depth, rows, wide),
        gx.reshape(chans, depth, rows, wide),
        gw.reshape(9, chans, co),
        gb.reshape(chans),
    )


def solution(mesh):
    placed = (P("ch", None, "xy", None), P(None, "ch", None), P("ch"), P("ch", None, "xy", None))
    return jax.shard_map(
        layer,
        mesh=mesh,
        in_specs=placed,
        out_specs=(
            P("ch", None, "xy", None),
            P("ch", None, "xy", None),
            P(None, "ch", None),
            P("ch"),
        ),
        check_vma=False,
    )
```

```python
import functools
import math

import jax
import jax.numpy as jnp
from jax import lax
from jax.experimental import pallas as pl
from jax.experimental.pallas import tpu as pltpu
from jax.sharding import PartitionSpec as P


def with_halo(shard, sides, width):
    for axis, dim in sides:
        devices, length = (lax.axis_size(axis), shard.shape[dim])
        up = [(i, (i + 1) % devices) for i in range(devices - 1)]
        down = [(j, i) for i, j in up]
        last = lax.slice_in_dim(shard, length - width, length, axis=dim)
        leading = lax.slice_in_dim(shard, 0, width, axis=dim)
        before = lax.ppermute(last, axis, up)
        after = lax.ppermute(leading, axis, down)
        shard = jnp.concatenate([before, shard, after], axis=dim)
    return shard


def tap_offsets():
    return [(a, b) for a in (-1, 0, 1) for b in (-1, 0, 1)]


def pad_columns(block):
    return jnp.pad(block, ((0, 0), (0, 0), (0, 0), (2, 2)))


def window_of(padded, a, b, rows, wide):
    count = padded.shape[0]
    return padded[:, :, 2 + 2 * a : 2 + 2 * a + rows, 2 + 2 * b : 2 + 2 * b + wide].reshape(
        count, -1
    )


def contract_lead(left, right):
    return lax.dot_general(
        left, right, (((0,), (0,)), ((), ())), preferred_element_type=jnp.float32
    )


def contract_last(left, right):
    return lax.dot_general(
        left, right, (((1,), (1,)), ((), ())), preferred_element_type=jnp.float32
    )


def activate(pre, cot_flat):
    output = jax.nn.gelu(pre, approximate=True).astype(jnp.bfloat16)
    _, pull = jax.vjp(lambda v: jax.nn.gelu(v, approximate=True), pre)
    grad_pre = pull(cot_flat.astype(jnp.float32))[0].astype(jnp.bfloat16)
    return (output, grad_pre)


def per_device(inputs, weight, bias, cotangent):
    chans, depth, rows, wide = inputs.shape
    out_local = bias.shape[0]
    cells = depth * rows * wide
    x_rim = with_halo(inputs, (("xy", 2),), 2)
    x_pad = pad_columns(x_rim)
    total = jnp.zeros((lax.axis_size("ch") * out_local, cells), jnp.float32)
    for t, (term_a, term_b) in enumerate(tap_offsets()):
        total = total + contract_lead(weight[t], window_of(x_pad, term_a, term_b, rows, wide))
    pre = lax.psum_scatter(
        total.reshape(lax.axis_size("ch") * out_local, depth, rows, wide),
        "ch",
        scatter_dimension=0,
        tiled=True,
    ).reshape(out_local, cells)
    pre = pre + bias[:, None]
    out_flat, grad_pre = activate(pre, cotangent.reshape(out_local, -1))
    g_rim = with_halo(grad_pre.reshape(out_local, depth, rows, wide), (("xy", 2),), 2)
    windows = [window_of(x_pad, a, b, rows, wide) for a, b in tap_offsets()]
    piece = lax.all_gather(g_rim, "ch", axis=0, tiled=True)
    grad_acc = jnp.zeros((chans, cells), jnp.float32)
    count = piece.shape[0]
    padded = pad_columns(piece)
    center = piece[:, :, 2 : 2 + rows, :].reshape(count, -1)
    pieces_w = []
    for t, (a, b) in enumerate(tap_offsets()):
        w_block = weight[t]
        g_win = padded[:, :, 2 - 2 * a : 2 - 2 * a + rows, 2 - 2 * b : 2 - 2 * b + wide].reshape(
            count, -1
        )
        grad_acc = grad_acc + jnp.dot(w_block, g_win, preferred_element_type=jnp.float32)
        pieces_w.append(contract_last(windows[t], center))
    fresh = jnp.stack(pieces_w, 0)
    grad_acc, grad_w = (grad_acc, fresh)
    grad_b = jnp.sum(grad_pre.astype(jnp.float32), axis=1)
    output = out_flat.reshape(out_local, depth, rows, wide)
    grad_x = grad_acc.astype(jnp.bfloat16).reshape(chans, depth, rows, wide)
    grad_w, grad_b = lax.psum((grad_w, grad_b), "xy")
    return (output, grad_x, grad_w, grad_b)


F32 = jnp.float32
BF16 = jnp.bfloat16
SLOPE = math.sqrt(2.0 / math.pi)
THIRDS = 3


def fused_kernel(
    nch, nxy, x_hbm, w_hbm, b_hbm, cot_hbm,
    out_ref, gx_ref, gw_ref, gb_ref,
    x_in, w_ref, b_ref, cot_in,
    xrow, crow, orow, x2d, xim, wp, pm, pf, pb, prv, g2d, sacc,
    gwf, csend, crecv, zsend, zrecv, fin,
    ls, xs, xr, ps, pr, gs, gr, hs, hr, cs, cr, zs, zr, as_, ar, fs, fr,
):
    cl, rows, wide = x_in.shape
    co = w_ref.shape[1]
    cells = rows * wide
    rim = 2 * wide
    kc = 9 * cl
    sub = cl // THIRDS
    tri = nch * sub
    me = lax.axis_index("ch")
    xy = lax.axis_index("xy")
    core = lax.rem(xy, 2)
    nz = nxy // 2
    z = xy // 2
    hrows = crecv.shape[1]
    shard = hrows // nz
    part = kc // 2
    partner = xy + 1 - 2 * core
    up = xy > 0
    down = xy < nxy - 1

    def peer(d):
        return lax.rem(me + d, nch)

    def zpeer(d):
        return lax.rem(z + d, nz) * 2 + core

    def remote(src, dst, ssem, rsem, **where):
        return pltpu.make_async_remote_copy(
            src_ref=src, dst_ref=dst, send_sem=ssem, recv_sem=rsem,
            device_id=where, device_id_type=pl.DeviceIdType.MESH,
        )

    loads = [
        pltpu.make_async_copy(src, dst, ls.at[i])
        for i, (src, dst) in enumerate(((x_hbm, x_in), (w_hbm, w_ref), (cot_hbm, cot_in), (b_hbm, b_ref)))
    ]
    for c in loads:
        c.start()

    barrier = pltpu.get_barrier_semaphore()
    for d in range(1, nch):
        pl.semaphore_signal(barrier, inc=1, device_id={"ch": peer(d)}, device_id_type=pl.DeviceIdType.MESH)
    for d in range(1, nxy):
        pl.semaphore_signal(
            barrier, inc=1, device_id={"xy": lax.rem(xy + d, nxy)}, device_id_type=pl.DeviceIdType.MESH
        )

    loads[0].wait()
    xrow[...] = x_in[...].astype(F32).reshape(cl * rows, wide)
    for r in range(rows):
        x2d[:, rim + r * wide : rim + (r + 1) * wide] = xrow[pl.ds(r, cl, stride=rows), :].astype(BF16)

    col = lax.broadcasted_iota(jnp.int32, (co, co), 1)
    rest = lax.rem(col, tri)
    target = lax.div(rest, sub) * cl + lax.div(col, tri) * sub + lax.rem(rest, sub)
    pm[...] = (lax.broadcasted_iota(jnp.int32, (co, co), 0) == target).astype(F32).astype(BF16)

    pl.semaphore_wait(barrier, nch - 1 + nxy - 1)

    to_up = remote(
        x2d.at[:, pl.ds(rim, rim)], x2d.at[:, pl.ds(rim + cells, rim)],
        xs.at[0], xr.at[0], xy=jnp.maximum(xy - 1, 0),
    )
    to_down = remote(
        x2d.at[:, pl.ds(cells, rim)], x2d.at[:, pl.ds(0, rim)],
        xs.at[1], xr.at[1], xy=jnp.minimum(xy + 1, nxy - 1),
    )
    pl.when(up)(to_up.start)
    pl.when(down)(to_down.start)

    loads[1].wait()
    wp[...] = jnp.dot(w_ref[...], pm[...], preferred_element_type=F32).astype(BF16)

    lane = lax.broadcasted_iota(jnp.int32, (cl, wide), 1)

    def spread(src_row):
        v = x2d[:, src_row * wide : (src_row + 1) * wide]
        vf = v.astype(F32)
        minus = jnp.where(lane >= 2, pltpu.roll(vf, 2, 1), 0.0).astype(BF16)
        plus = jnp.where(lane < wide - 2, pltpu.roll(vf, wide - 2, 1), 0.0).astype(BF16)
        for a in (-1, 0, 1):
            r = src_row - 2 - 2 * a
            if 0 <= r < rows:
                for b, val in ((-1, minus), (0, v), (1, plus)):
                    t = 3 * (a + 1) + b + 1
                    xim[t * cl : (t + 1) * cl, r * wide : (r + 1) * wide] = val

    for src_row in range(2, rows + 2):
        spread(src_row)
    xim[kc:, :] = jnp.ones((xim.shape[0] - kc, cells), BF16)

    def edge_zero(cond, ref, start):
        @pl.when(jnp.logical_not(cond))
        def _():
            ref[:, start : start + rim] = jnp.zeros((ref.shape[0], rim), BF16)

    edge_zero(up, x2d, 0)
    edge_zero(down, x2d, rim + cells)
    edge_zero(up, g2d, 0)
    edge_zero(down, g2d, rim + cells)

    loads[2].wait()
    loads[3].wait()
    crow[...] = cot_in[...].astype(F32).reshape(cl * rows, wide)
    eye = lax.broadcasted_iota(jnp.int32, (cl, cl), 0) == lax.broadcasted_iota(jnp.int32, (cl, cl), 1)
    bias = jnp.sum(jnp.where(eye, jnp.broadcast_to(b_ref[...], (cl, cl)), 0.0), axis=1, keepdims=True)

    pl.when(up)(to_down.wait_recv)
    pl.when(down)(to_up.wait_recv)
    for src_row in (0, 1, rows + 2, rows + 3):
        spread(src_row)

    def block(q, j):
        return pl.ds(pl.multiple_of(q * tri + j * sub, 16), sub)

    sends = []
    psends = {}
    gsends = {}
    hsends = {}
    ccopies = {}
    zcopies = {}
    acopies = {}
    fcopies = {}

    def forward(q):
        rs = slice(q * tri, (q + 1) * tri)
        val = contract_lead(wp[:, rs], xim[:kc, :])
        pf[rs, :] = val
        pb[rs, :] = val.astype(BF16)

    def send_partial(q):
        for d in range(1, nch):
            k = q * (nch - 1) + d - 1
            c = remote(pb.at[block(q, peer(d)), :], prv.at[k], ps.at[k], pr.at[k], ch=peer(d))
            c.start()
            psends[(q, d)] = c

    def activation(q):
        for d in range(1, nch):
            psends[(q, d)].wait_recv()
        if q == 1:
            send_partial(2)
        mine = block(q, me)
        for r in range(rows):
            rc = pl.ds(r * wide, wide)
            v = pf[mine, rc] + bias[q * sub : (q + 1) * sub]
            for d in range(1, nch):
                v = v + prv[q * (nch - 1) + d - 1, :, rc].astype(F32)
            sq = v * v
            th = jnp.tanh(SLOPE * (v + 0.044715 * (sq * v)))
            hp = 0.5 * (1.0 + th)
            spot = pl.ds(q * sub * rows + r, sub, stride=rows)
            orow[spot, :] = v * hp
            slope = hp + 0.5 * v * (1.0 - th * th) * (SLOPE * (1.0 + 3.0 * 0.044715 * sq))
            g2d[mine, pl.ds(rim + r * wide, wide)] = (crow[spot, :] * slope).astype(BF16)
        blk = g2d.at[mine, pl.ds(rim, cells)]
        for d in range(1, nch):
            k = q * (nch - 1) + d - 1
            c = remote(blk, blk, gs.at[k], gr.at[k], ch=peer(d))
            c.start()
            gsends[(q, d)] = c
            sends.append(c)

    def kernel_grad(q):
        for d in range(1, nch):
            gsends[(q, d)].wait_recv()
        rs = pl.ds(q * tri, tri)
        c = remote(
            g2d.at[rs, pl.ds(rim, rim)], g2d.at[rs, pl.ds(rim + cells, rim)],
            hs.at[2 * q], hr.at[2 * q], xy=jnp.maximum(xy - 1, 0),
        )
        pl.when(up)(c.start)
        hsends[(q, 0)] = c
        c = remote(
            g2d.at[rs, pl.ds(cells, rim)], g2d.at[rs, pl.ds(0, rim)],
            hs.at[2 * q + 1], hr.at[2 * q + 1], xy=jnp.minimum(xy + 1, nxy - 1),
        )
        pl.when(down)(c.start)
        hsends[(q, 1)] = c
        gwf[q] = contract_last(xim[...], g2d[rs, rim : rim + cells])
        theirs = pl.ds(pl.multiple_of((1 - core) * part, 16), hrows)
        csend[q] = gwf[q, theirs, :].astype(BF16)
        c = remote(csend.at[q], crecv.at[q], cs.at[q], cr.at[q], xy=partner)
        c.start()
        ccopies[q] = c
        sends.append(c)

    def scatter_z(q):
        ccopies[q].wait_recv()
        mine = pl.ds(pl.multiple_of(core * part, 16), hrows)
        val = gwf[q, mine, :] + crecv[q].astype(F32)
        gwf[q, mine, :] = val
        zsend[q] = val.astype(BF16)
        for d in range(1, nz):
            k = q * (nz - 1) + d - 1
            at = pl.ds(pl.multiple_of(lax.rem(z + d, nz) * shard, 16), shard)
            c = remote(zsend.at[q, at, :], zrecv.at[k], zs.at[k], zr.at[k], xy=zpeer(d))
            c.start()
            zcopies[(q, d)] = c
            sends.append(c)

    def gather_z(q):
        total = gwf[q, pl.ds(pl.multiple_of(core * part + z * shard, 16), shard), :]
        for d in range(1, nz):
            zcopies[(q, d)].wait_recv()
            total = total + zrecv[q * (nz - 1) + d - 1].astype(F32)
        at = pl.ds(pl.multiple_of(z * shard, 16), shard)
        fin[q, core, at, :] = total.astype(BF16)
        blk = fin.at[q, core, at, :]
        for d in range(1, nz):
            k = q * (nz - 1) + d - 1
            c = remote(blk, blk, as_.at[k], ar.at[k], xy=zpeer(d))
            c.start()
            acopies[(q, d)] = c
            sends.append(c)
        c = remote(blk, blk, fs.at[q * nz], fr.at[q * nz], xy=partner)
        c.start()
        fcopies[(q, 0)] = c
        sends.append(c)

    def gather_core(q):
        for d in range(1, nz):
            acopies[(q, d)].wait_recv()
            at = pl.ds(pl.multiple_of(lax.rem(z - d + nz, nz) * shard, 16), shard)
            blk = fin.at[q, core, at, :]
            c = remote(blk, blk, fs.at[q * nz + d], fr.at[q * nz + d], xy=partner)
            c.start()
            fcopies[(q, d)] = c
            sends.append(c)

    def finish(q):
        for d in range(nz):
            fcopies[(q, d)].wait_recv()
        back = pm[:, q * tri : (q + 1) * tri]
        for h in range(2):
            val = contract_last(fin[q, h, :part, :], back)
            if q == 0:
                gw_ref[h * part : (h + 1) * part, :] = val
            else:
                gw_ref[h * part : (h + 1) * part, :] += val
        i = lax.broadcasted_iota(jnp.int32, (tri, wide), 0) - me * sub
        j = lax.broadcasted_iota(jnp.int32, (tri, wide), 1) - q * sub
        pick = ((i == j) & (j >= 0) & (j < sub)).astype(F32).astype(BF16)
        gb = jnp.dot(fin[q, 1, part:, :], pick, preferred_element_type=F32)[0:1, :cl]
        if q == 0:
            gb_ref[...] = gb
        else:
            gb_ref[...] += gb

    pairs = rows // 2
    group = 3 * cl
    seen = set()

    def gi_chunk(k):
        val = jnp.dot(wp[...], g2d[:, k * rim : (k + 1) * rim], preferred_element_type=F32)
        for a in (-1, 0, 1):
            p = k - 1 + a
            if 0 <= p < pairs:
                piece = val[(a + 1) * group : (a + 2) * group]
                if p in seen:
                    sacc[:, p * rim : (p + 1) * rim] += piece
                else:
                    seen.add(p)
                    sacc[:, p * rim : (p + 1) * rim] = piece

    forward(0)
    send_partial(0)
    forward(1)
    forward(2)
    for d in range(1, nch):
        psends[(0, d)].wait_send()
    send_partial(1)
    activation(0)
    activation(1)
    for d in range(1, nch):
        psends[(1, d)].wait_send()
    kernel_grad(0)
    scatter_z(0)
    activation(2)
    for d in range(1, nch):
        psends[(2, d)].wait_send()
    out_ref[...] = orow[...].reshape(cl, rows, wide).astype(BF16)
    gather_z(0)
    kernel_grad(1)
    scatter_z(1)
    gather_core(0)
    kernel_grad(2)
    scatter_z(2)
    finish(0)
    gather_z(1)
    for q in range(THIRDS):
        pl.when(up)(hsends[(q, 1)].wait_recv)
        pl.when(down)(hsends[(q, 0)].wait_recv)
    for k in range(pairs + 2):
        gi_chunk(k)
    gather_core(1)
    gather_z(2)
    for r in range(rows):
        rc = slice(r * wide, (r + 1) * wide)
        v = sacc[cl : 2 * cl, rc]
        v = v + jnp.where(lane < wide - 2, pltpu.roll(sacc[:cl, rc], wide - 2, 1), 0.0)
        v = v + jnp.where(lane >= 2, pltpu.roll(sacc[2 * cl :, rc], 2, 1), 0.0)
        xrow[pl.ds(r, cl, stride=rows), :] = v
    gx_ref[...] = xrow[...].reshape(cl, rows, wide).astype(BF16)
    finish(1)
    gather_core(2)
    finish(2)

    pl.when(up)(to_up.wait_send)
    pl.when(down)(to_down.wait_send)
    for q in range(THIRDS):
        pl.when(up)(hsends[(q, 0)].wait_send)
        pl.when(down)(hsends[(q, 1)].wait_send)
    for c in sends:
        c.wait_send()


def fits(chans, depth, rows, wide, co, nch, nxy):
    part = 9 * chans // 2
    return (
        depth == 1
        and rows % 4 == 0
        and wide == 128
        and chans % (32 * THIRDS) == 0
        and chans <= wide
        and co == nch * chans
        and (nch * chans) % (THIRDS * 128) == 0
        and nxy % 2 == 0
        and (part + 16) % (16 * (nxy // 2)) == 0
    )


def layer(inputs, weight, bias, cotangent):
    chans, depth, rows, wide = inputs.shape
    nch, nxy = lax.axis_size("ch"), lax.axis_size("xy")
    co = weight.shape[2]
    if not fits(chans, depth, rows, wide, co, nch, nxy):
        return per_device(inputs, weight, bias, cotangent)
    cells = rows * wide
    kc = 9 * chans
    nz = nxy // 2
    hrows = kc // 2 + 16
    sub = chans // THIRDS
    tri = nch * sub
    dma = pltpu.SemaphoreType.DMA
    vmem = pltpu.VMEM
    sems = (
        [4, 2, 2]
        + [THIRDS * (nch - 1)] * 4
        + [2 * THIRDS] * 2
        + [THIRDS] * 2
        + [THIRDS * (nz - 1)] * 4
        + [THIRDS * nz] * 2
    )
    out, gx, gw, gb = pl.pallas_call(
        functools.partial(fused_kernel, nch, nxy),
        out_shape=(
            jax.ShapeDtypeStruct((chans, rows, wide), BF16),
            jax.ShapeDtypeStruct((chans, rows, wide), BF16),
            jax.ShapeDtypeStruct((kc, co), F32),
            jax.ShapeDtypeStruct((1, chans), F32),
        ),
        in_specs=[pl.BlockSpec(memory_space=pltpu.HBM)] * 4,
        out_specs=[pl.BlockSpec(memory_space=vmem)] * 4,
        scratch_shapes=[
            vmem((chans, rows, wide), BF16),
            vmem((kc, co), BF16),
            vmem((1, chans), F32),
            vmem((chans, rows, wide), BF16),
            vmem((chans * rows, wide), F32),
            vmem((chans * rows, wide), F32),
            vmem((chans * rows, wide), F32),
            vmem((chans, cells + 4 * wide), BF16),
            vmem((kc + 16, cells), BF16),
            vmem((kc, co), BF16),
            vmem((co, co), BF16),
            vmem((co, cells), F32),
            vmem((co, cells), BF16),
            vmem((THIRDS * (nch - 1), sub, cells), BF16),
            vmem((co, cells + 4 * wide), BF16),
            vmem((3 * chans, cells), F32),
            vmem((THIRDS, kc + 16, tri), F32),
            vmem((THIRDS, hrows, tri), BF16),
            vmem((THIRDS, hrows, tri), BF16),
            vmem((THIRDS, hrows, tri), BF16),
            vmem((THIRDS * (nz - 1), hrows // nz, tri), BF16),
            vmem((THIRDS, 2, hrows, tri), BF16),
        ]
        + [dma((n,)) for n in sems],
        compiler_params=pltpu.CompilerParams(
            collective_id=0, has_side_effects=True, vmem_limit_bytes=60 * 1024 * 1024
        ),
    )(
        inputs.reshape(chans, rows, wide),
        weight.reshape(kc, co),
        bias.reshape(1, chans),
        cotangent.reshape(chans, rows, wide),
    )
    return (
        out.reshape(chans, depth, rows, wide),
        gx.reshape(chans, depth, rows, wide),
        gw.reshape(9, chans, co),
        gb.reshape(chans),
    )


def solution(mesh):
    placed = (P("ch", None, "xy", None), P(None, "ch", None), P("ch"), P("ch", None, "xy", None))
    return jax.shard_map(
        layer,
        mesh=mesh,
        in_specs=placed,
        out_specs=(
            P("ch", None, "xy", None),
            P("ch", None, "xy", None),
            P(None, "ch", None),
            P("ch"),
        ),
        check_vma=False,
    )
```
